256 devices in a mesh: dom: 32 (over z, y), feat: 8 (over x, core).
Axes of the slice: x: 4, y: 4, z: 8, core: 2. Of those that a mesh axis runs over, the one named last changes fastest.
Arguments:
- features: bfloat16 [8192, 8, 25088], P('dom', 'feat'), may hold values from -50 to 50, as said below
- weights: float32 [8, 32, 25088], P('feat', None, 'dom'), may hold values from -6 to 6
- geno_live: int32 [4], replicated, may hold values from 1 to 25088, 100000 in all
- image_live: int32 [4], replicated, may hold values from 1 to 12544, 50000 in all
Outputs:
- updated: float32 [8, 32, 25088], P('feat', None, 'dom')
The draws below stay inside these ranges and needn't reach their ends.
Inputs may be any that keep to these rules, and one draw needn't show every extreme that they name: `features`: rows are participants; every entry is finite. `geno_live`: the counts sum to 100000. `image_live`: the counts sum to 50000.
All inputs are finite; a program needn't handle non-finite values.
Results may differ from the reference program's by a relative error of at most 0.0048.
Values may be sent and summed in bfloat16 or wider, within the bound.
No kernel may reach another device: no remote copies, remote signals or barrier semaphores. Data moves between devices by JAX's collectives and lax.ppermute only.
A program may use at most 64 MiB of HBM per device.

```python
import math
import jax
import jax.numpy as jnp
import numpy as np
from jax import lax

GX = 100000
GY = 50000
K = 32
ITERS = 2
SUBJECTS = 8192
FB = 25088
N_FEAT = 8


def draw_features(key, part):
    key = jax.random.fold_in(key, 11)
    key_base, key_rows, key_cols = jax.random.split(key, 3)
    shape = (SUBJECTS, N_FEAT, FB)
    position = jnp.arange(SUBJECTS, dtype=jnp.float32) / SUBJECTS
    base = jax.random.truncated_normal(key_base, -4.0, 4.0, shape, jnp.float32)
    row_power = -0.5 + 0.5 * position + 0.5 * jax.random.uniform(key_rows, (SUBJECTS,), jnp.float32)
    col_power = jax.random.uniform(key_cols, (N_FEAT, FB), jnp.float32, -0.5, 0.5)
    scaled = base * (10.0 ** row_power)[:, None, None] * (10.0 ** col_power)[None, :, :]
    return scaled.astype(jnp.bfloat16)


def block_levels(rng, dims, cuts, smallest, top_value):
    gain, own = 1.0, jax.random.fold_in(rng, 6)
    for dim, blocks in cuts:
        steps = jnp.exp(jax.random.uniform(jax.random.fold_in(own, dim), (blocks,), jnp.float32, smallest / len(cuts), top_value / len(cuts)))
        gain = gain * jnp.repeat(steps, dims[dim] // blocks).reshape([-1 if axis == dim else 1 for axis in range(len(dims))])
    return gain


def profile(amount, total, limit, slope):
    portions = [(1 << 20) // math.isqrt(grade ** slope) + 1 for grade in range(2, amount + 1)]
    spare, holding = total - limit - (amount - 1), [1] * (amount - 1)
    while spare > 0:
        candidates = [i for i in range(amount - 1) if holding[i] < limit]
        mass, remaining = sum([portions[i] for i in candidates]), spare
        for i in candidates:
            more = min(limit - holding[i], max(1, remaining * portions[i] // mass), spare)
            holding[i] = holding[i] + more
            spare = spare - more
    return np.array([limit] + holding)


def ragged_sizes(rng, count, total, limit, skew):
    if count == 2:
        one = jax.random.randint(rng, (), max(1, total - limit), min(limit, total - 1) + 1)
        return jnp.stack([one, total - one])
    lengths = jnp.asarray(profile(count, total, limit, skew), jnp.int32)
    pairs = (count - 1) // 2
    giver, sink = lengths[1:1 + 2 * pairs:2], lengths[2:2 + 2 * pairs:2]
    room = jnp.minimum(giver - 1, limit - sink)
    shifted = jax.random.randint(jax.random.fold_in(rng, 1), (pairs,), 0, 1 << 20) % (room + 1)
    lengths = lengths.at[1:1 + 2 * pairs:2].set(giver - shifted).at[2:2 + 2 * pairs:2].set(sink + shifted)
    return lengths[jax.random.permutation(jax.random.fold_in(rng, 2), count)]


def bell_draw(key, dims, scale, reach, pieces=(), kind=jnp.bfloat16):
    factor_of = block_levels(key, dims, pieces, -0.22, 0.18) if pieces else 1.0
    entries = jax.random.normal(key, dims, jnp.float32) * scale * factor_of
    return jnp.minimum(jnp.maximum(entries, -reach), reach).astype(kind)


def setup_inputs(seed: int = 0) -> dict:
    seeds = jax.random.split(jax.random.key(seed), 5)
    return {
        "features": draw_features(jax.random.fold_in(seeds[4], 71), 0),
        "weights": bell_draw(seeds[1], (N_FEAT, K, FB), 1.0, 6.0, ((0, 8), (2, 32)), jnp.float32),
        "geno_live": ragged_sizes(seeds[2], N_FEAT // 2, GX, FB, 0).astype(jnp.int32),
        "image_live": ragged_sizes(seeds[3], N_FEAT // 2, GY, FB // 2, 0).astype(jnp.int32),
    }


step_rate = 0.1
jitter = 1e-05

def whiten_partner(factor, partner):
    return jax.scipy.linalg.solve_triangular(factor, partner.T, lower=True).T

def reference(features, weights, geno_live, image_live):
    half_feat = N_FEAT // 2
    live = jnp.concatenate([geno_live, image_live]).astype(jnp.int32)
    mask = (jnp.arange(FB, dtype=jnp.int32)[None, :] < live[:, None]).astype(jnp.float32)
    identity = jnp.eye(K, dtype=jnp.float32)
    blocks = jnp.arange(N_FEAT, dtype=jnp.int32)
    current = weights
    for sweep in range(ITERS):
        rounded = (current * mask[:, None, :]).astype(jnp.bfloat16)

        def project(index):
            block = lax.dynamic_index_in_dim(features, index, 1, False)
            weight_piece = lax.dynamic_index_in_dim(rounded, index, 0, False)
            return lax.dot_general(block.astype(jnp.float32), weight_piece.astype(jnp.float32), (((1,), (1,)), ((), ())), preferred_element_type=jnp.float32)
        partial_value = lax.map(project, blocks)
        geno_proj = jnp.sum(partial_value[:half_feat], axis=0) * GX ** (-0.5)
        image_proj = jnp.sum(partial_value[half_feat:], axis=0) * GY ** (-0.5)
        projected = jnp.stack([geno_proj, image_proj])
        gram_total = jnp.einsum('vrk,vrl->vkl', projected, projected, precision=lax.Precision.HIGHEST)
        factor = jnp.linalg.cholesky(gram_total / SUBJECTS + jitter * identity)
        geno_target = whiten_partner(factor[1], image_proj)
        image_target = whiten_partner(factor[0], geno_proj)
        geno_resid = (geno_proj - geno_target).astype(jnp.bfloat16)
        image_resid = (image_proj - image_target).astype(jnp.bfloat16)

        def gradient_block(index):
            block = lax.dynamic_index_in_dim(features, index, 1, False)
            residual_rows = jnp.where(index < half_feat, geno_resid, image_resid)
            return lax.dot_general(residual_rows.astype(jnp.float32), block.astype(jnp.float32), (((0,), (0,)), ((), ())), preferred_element_type=jnp.float32)
        gradient = lax.map(gradient_block, blocks)
        current = mask[:, None, :] * (current - step_rate * SUBJECTS ** (-0.5) * gradient)
    return current
```

```python
import functools
import jax
import jax.numpy as jnp
from jax import lax
from jax.experimental import pallas as pl
from jax.experimental.pallas import tpu as pltpu
from jax.sharding import PartitionSpec as P

GX = 100000
GY = 50000
K = 32
ITERS = 2
LANES = 128
step_rate = 0.1
jitter = 1e-05

VMEM = pl.BlockSpec(memory_space=pltpu.VMEM)
SMEM = pl.BlockSpec(memory_space=pltpu.SMEM)
PARAMS = pltpu.CompilerParams(vmem_limit_bytes=48 * 1024 * 1024)
HIGH = lax.Precision.HIGHEST
F32 = jnp.float32
BF16 = jnp.bfloat16


def window(width):
    return -(-(width + LANES - 16) // LANES) * LANES


def base_of(index, width):
    return (index * width) // LANES * LANES


def lane_mask(info, width):
    column = lax.broadcasted_iota(jnp.int32, (K, width), 1) + info[1] * width
    return (column < info[0]).astype(F32)


def spread(info, masked, width, pad, copies):
    pad[...] = jnp.zeros(pad.shape, F32)
    pad[:, :width] = masked
    shift = lax.rem(info[1] * width, LANES)
    rounded = pltpu.roll(pad[...], shift, 1).astype(BF16)
    for copy in range(copies.shape[0]):
        copies[copy] = rounded


def first_kernel(info, weights, copies, pad):
    width = weights.shape[1]
    spread(info, weights[...] * lane_mask(info, width), width, pad, copies)


def project_kernel(windows, features, copies, full):
    count, _, size = windows.shape
    width = features.shape[1] // count
    full[...] = jnp.zeros(full.shape, BF16)
    for shard in range(count):
        base = base_of(shard, width)
        full[:, base : base + size] += windows[shard]
    partial = lax.dot_general(
        features[...], full[...], (((1,), (1,)), ((), ())), preferred_element_type=F32
    ).T
    for copy in range(copies.shape[0]):
        copies[copy] = partial


def gram_kernel(info, partials, own, partner, copies):
    half = partials.shape[0] // 2
    geno = partials[0]
    image = partials[half]
    for block in range(1, half):
        geno += partials[block]
        image += partials[half + block]
    geno *= GX ** (-0.5)
    image *= GY ** (-0.5)
    is_geno = info[2] == 1
    own[...] = jnp.where(is_geno, geno, image)
    other = jnp.where(is_geno, image, geno)
    partner[...] = other
    tiled = jnp.concatenate([other] * (LANES // K), axis=0)
    gram = lax.dot_general(
        other, tiled, (((1,), (1,)), ((), ())), precision=HIGH, preferred_element_type=F32
    )
    lane = lax.broadcasted_iota(jnp.int32, (8, LANES), 1)
    packed = jnp.zeros((8, LANES), F32)
    for part in range(LANES // K):
        packed = jnp.where(lane // K == part, gram[8 * part : 8 * part + 8], packed)
    for copy in range(copies.shape[0]):
        copies[copy] = packed


def residual_kernel(participants, grams, own, partner, features, windows):
    total = grams[0]
    for part in range(1, grams.shape[0]):
        total += grams[part]
    rows = [total] + [pltpu.roll(total, LANES - K * part, 1) for part in range(1, LANES // K)]
    row = lax.broadcasted_iota(jnp.int32, (K, LANES), 0)
    lane = lax.broadcasted_iota(jnp.int32, (K, LANES), 1)
    covariance = jnp.concatenate(rows, axis=0) / participants
    covariance += jnp.where(lane == row, jitter, 0.0)
    state = jnp.where(lane < K, covariance, jnp.where(lane == row + K, 1.0, 0.0))
    pivots = jnp.zeros((K, 1), F32)
    for step in range(K):
        pivot_row = state[step : step + 1, :]
        column = state[:, step : step + 1]
        pivot = pivot_row[:, step : step + 1]
        pivots = jnp.where(row[:, :1] == step, pivot, pivots)
        ratio = jnp.where(row[:, :1] > step, column / pivot, 0.0)
        state = state - ratio * pivot_row
    scaled = state * lax.rsqrt(pivots)
    inverse = pltpu.roll(scaled, LANES - K, 1)[:, :K]
    target = lax.dot_general(
        inverse, partner[...], (((1,), (0,)), ((), ())), precision=HIGH, preferred_element_type=F32
    )
    residual = (own[...] - target).astype(BF16)
    count, _, size = windows.shape
    width = features.shape[1] // count
    for shard in range(count):
        base = base_of(shard, width)
        windows[shard] = lax.dot_general(
            residual,
            features[:, base : base + size],
            (((1,), (0,)), ((), ())),
            preferred_element_type=F32,
        ).astype(BF16)


def updated_weights(step_size, info, windows, weights):
    width = weights.shape[1]
    total = windows[0].astype(F32)
    for part in range(1, windows.shape[0]):
        total += windows[part].astype(F32)
    size = windows.shape[2]
    shift = lax.rem(size - lax.rem(info[1] * width, LANES), size)
    gradient = pltpu.roll(total, shift, 1)[:, :width]
    return lane_mask(info, width) * (weights[...] - step_size * gradient)


def update_kernel(step_size, info, windows, weights, updated, copies, pad):
    width = weights.shape[1]
    fresh = updated_weights(step_size, info, windows, weights)
    updated[...] = fresh
    spread(info, fresh, width, pad, copies)


def last_kernel(step_size, info, windows, weights, updated):
    updated[...] = updated_weights(step_size, info, windows, weights)


def call(kernel, outs, scratch=(), specs=None):
    shapes = tuple(jax.ShapeDtypeStruct(*out) for out in outs)
    return pl.pallas_call(
        kernel,
        out_shape=shapes,
        in_specs=specs,
        out_specs=tuple(VMEM for _ in shapes),
        scratch_shapes=list(scratch),
        compiler_params=PARAMS,
    )


def exchange(copies, axis):
    return lax.all_to_all(copies, axis, 0, 0, tiled=True)


def body(features, weights, geno_live, image_live):
    row_count = features.shape[0]
    own_block = features[:, 0, :]
    current = weights[0]
    width = current.shape[1]
    size = window(width)
    doms = lax.axis_size("dom")
    feats = lax.axis_size("feat")
    participants = row_count * doms
    half = feats // 2
    feat = lax.axis_index("feat")
    lives = jnp.concatenate([geno_live, image_live])
    live_count = jnp.sum(jnp.where(jnp.arange(feats) == feat, lives, 0))
    info = jnp.stack([live_count, lax.axis_index("dom"), (feat < half).astype(jnp.int32)])
    step_size = step_rate * participants ** (-0.5)

    pad = pltpu.VMEM((K, size), F32)
    spread_out = ((doms, K, size), BF16)
    (copies,) = call(first_kernel, [spread_out], [pad], [SMEM, VMEM])(info, current)
    for sweep in range(ITERS):
        (copies,) = call(
            project_kernel,
            [((feats, K, row_count), F32)],
            [pltpu.VMEM((K, own_block.shape[1]), BF16)],
            [VMEM, VMEM],
        )(exchange(copies, "dom"), own_block)
        own, partner, copies = call(
            gram_kernel,
            [((K, row_count), F32), ((K, row_count), F32), ((doms, 8, LANES), F32)],
            (),
            [SMEM, VMEM],
        )(info, exchange(copies, "feat"))
        (copies,) = call(
            functools.partial(residual_kernel, participants), [spread_out], (), [VMEM] * 4
        )(exchange(copies, "dom"), own, partner, own_block)
        shares = exchange(copies, "dom")
        if sweep < ITERS - 1:
            current, copies = call(
                functools.partial(update_kernel, step_size),
                [(current.shape, F32), spread_out],
                [pad],
                [SMEM, VMEM, VMEM],
            )(info, shares, current)
        else:
            (current,) = call(
                functools.partial(last_kernel, step_size),
                [(current.shape, F32)],
                (),
                [SMEM, VMEM, VMEM],
            )(info, shares, current)
    return current[None]


def solution(mesh):
    placed = (P("dom", "feat", None), P("feat", None, "dom"), P(), P())
    return jax.shard_map(
        body, mesh=mesh, in_specs=placed, out_specs=P("feat", None, "dom"), check_vma=False
    )
```

```python
import functools
import jax
import jax.numpy as jnp
from jax import lax
from jax.experimental import pallas as pl
from jax.experimental.pallas import tpu as pltpu
from jax.sharding import Mesh
from jax.sharding import PartitionSpec as P

GX = 100000
GY = 50000
K = 32
ITERS = 2
LANES = 128
NEAR = 8
step_rate = 0.1
jitter = 1e-05

VMEM = pl.BlockSpec(memory_space=pltpu.VMEM)
SMEM = pl.BlockSpec(memory_space=pltpu.SMEM)
SMALL = 24 * 1024 * 1024
LARGE = 60 * 1024 * 1024
HIGH = lax.Precision.HIGHEST
F32 = jnp.float32
BF16 = jnp.bfloat16


def padded(width):
    return -(-width // LANES) * LANES


def window(width):
    return padded(width + LANES - 16)


def base_of(index, width):
    return (index * width) // LANES * LANES


def offset_of(index, width):
    return lax.rem(index * width, LANES)


def at_offset(values, index, width):
    lane = lax.broadcasted_iota(jnp.int32, values.shape, 1)
    begin = (index * width) % LANES
    return jnp.where((lane >= begin) & (lane < begin + width), values, 0.0)


def moved(values, source, target, width):
    size = values.shape[1]
    shift = ((target * width) % LANES - (source * width) % LANES) % size
    values = at_offset(values, source, width)
    return pltpu.roll(values, shift, 1) if shift else values


def is_geno():
    return lax.axis_index("feat") < lax.axis_size("feat") // 2


def lane_mask(geno_live, image_live, width):
    slot = lax.rem(lax.axis_index("feat"), lax.axis_size("feat") // 2)
    live = jnp.where(is_geno(), geno_live[slot], image_live[slot])
    shard = lax.axis_index("far") * NEAR + lax.axis_index("near")
    column = lax.broadcasted_iota(jnp.int32, (K, width), 1) + shard * width
    return (column < live).astype(F32)


def spread(masked, width, pad, copies):
    pad[...] = jnp.zeros(pad.shape, F32)
    pad[:, :width] = masked
    shift = offset_of(lax.axis_index("far"), width)
    rounded = pltpu.roll(pad[...], shift, 1).astype(BF16)
    for copy in range(copies.shape[0]):
        copies[copy] = rounded


def first_kernel(geno_live, image_live, weights, copies, pad):
    width = weights.shape[1]
    masked = weights[...] * lane_mask(geno_live, image_live, width)
    spread(masked, width, pad, copies)


def join_kernel(width, windows, copies):
    size = windows.shape[2]
    first = copies.at[0]
    first[...] = jnp.zeros(first.shape, BF16)
    for part in range(windows.shape[0]):
        base = base_of(part, width)
        first[:, base : base + size] += windows[part]
    for copy in range(1, copies.shape[0]):
        copies[copy] = first[...]


def project_kernel(far, joined, features, copies, full):
    near = joined.shape[0]
    width = features.shape[1] // (far * near)
    size = window(width)
    full[...] = jnp.zeros(full.shape, BF16)
    for part in range(far):
        start = base_of(part, width)
        for source in range(near):
            piece = joined[source, :, start : start + size].astype(F32)
            base = base_of(part * near + source, width)
            full[:, base : base + size] += moved(piece, part, source, width).astype(BF16)
    partial = lax.dot_general(
        features[...], full[...], (((1,), (1,)), ((), ())), preferred_element_type=F32
    ).T
    for copy in range(copies.shape[0]):
        copies[copy] = partial


def gram_kernel(partials, own, partner, copies):
    half = partials.shape[0] // 2
    geno = partials[0]
    image = partials[half]
    for block in range(1, half):
        geno += partials[block]
        image += partials[half + block]
    geno *= GX ** (-0.5)
    image *= GY ** (-0.5)
    own[...] = jnp.where(is_geno(), geno, image)
    other = jnp.where(is_geno(), image, geno)
    partner[...] = other
    tiled = jnp.concatenate([other] * (LANES // K), axis=0)
    gram = lax.dot_general(
        other, tiled, (((1,), (1,)), ((), ())), precision=HIGH, preferred_element_type=F32
    )
    lane = lax.broadcasted_iota(jnp.int32, (8, LANES), 1)
    packed = jnp.zeros((8, LANES), F32)
    for part in range(LANES // K):
        packed = jnp.where(lane // K == part, gram[8 * part : 8 * part + 8], packed)
    for copy in range(copies.shape[0]):
        copies[copy] = packed


def residual_kernel(participants, far, grams, own, partner, features, joined, total_row):
    total = grams[0]
    for part in range(1, grams.shape[0]):
        total += grams[part]
    rows = [total] + [pltpu.roll(total, LANES - K * part, 1) for part in range(1, LANES // K)]
    row = lax.broadcasted_iota(jnp.int32, (K, LANES), 0)
    lane = lax.broadcasted_iota(jnp.int32, (K, LANES), 1)
    covariance = jnp.concatenate(rows, axis=0) / participants
    covariance += jnp.where(lane == row, jitter, 0.0)
    state = jnp.where(lane < K, covariance, jnp.where(lane == row + K, 1.0, 0.0))
    pivots = jnp.zeros((K, 1), F32)
    for step in range(K):
        pivot_row = state[step : step + 1, :]
        column = state[:, step : step + 1]
        pivot = pivot_row[:, step : step + 1]
        pivots = jnp.where(row[:, :1] == step, pivot, pivots)
        ratio = jnp.where(row[:, :1] > step, column / pivot, 0.0)
        state = state - ratio * pivot_row
    scaled = state * lax.rsqrt(pivots)
    inverse = pltpu.roll(scaled, LANES - K, 1)[:, :K]
    target = lax.dot_general(
        inverse, partner[...], (((1,), (0,)), ((), ())), precision=HIGH, preferred_element_type=F32
    )
    residual = (own[...] - target).astype(BF16)
    near = joined.shape[0]
    width = features.shape[1] // (far * near)
    size = window(width)
    for target_index in range(near):
        total_row[...] = jnp.zeros(total_row.shape, F32)
        for part in range(far):
            base = base_of(part * near + target_index, width)
            piece = lax.dot_general(
                residual,
                features[:, base : base + size],
                (((1,), (0,)), ((), ())),
                preferred_element_type=F32,
            )
            start = base_of(part, width)
            total_row[:, start : start + size] += moved(piece, target_index, part, width)
        joined[target_index] = total_row[...].astype(BF16)


def fold_kernel(width, joined, windows):
    total = joined[0].astype(F32)
    for source in range(1, joined.shape[0]):
        total += joined[source].astype(F32)
    total = total.astype(BF16)
    size = windows.shape[2]
    for part in range(windows.shape[0]):
        start = base_of(part, width)
        windows[part] = total[:, start : start + size]


def updated_weights(step_size, geno_live, image_live, windows, weights):
    width = weights.shape[1]
    total = windows[0].astype(F32)
    for part in range(1, windows.shape[0]):
        total += windows[part].astype(F32)
    size = windows.shape[2]
    shift = lax.rem(size - offset_of(lax.axis_index("far"), width), size)
    gradient = pltpu.roll(total, shift, 1)[:, :width]
    return lane_mask(geno_live, image_live, width) * (weights[...] - step_size * gradient)


def update_kernel(step_size, geno_live, image_live, windows, weights, updated, copies, pad):
    fresh = updated_weights(step_size, geno_live, image_live, windows, weights)
    updated[...] = fresh
    spread(fresh, weights.shape[1], pad, copies)


def last_kernel(step_size, geno_live, image_live, windows, weights, updated):
    updated[...] = updated_weights(step_size, geno_live, image_live, windows, weights)


def call(kernel, outs, scratch, specs, *operands, grant=SMALL):
    shapes = tuple(jax.ShapeDtypeStruct(*out) for out in outs)
    return pl.pallas_call(
        kernel,
        out_shape=shapes,
        in_specs=specs,
        out_specs=tuple(VMEM for _ in shapes),
        scratch_shapes=list(scratch),
        compiler_params=pltpu.CompilerParams(vmem_limit_bytes=grant),
    )(*operands)


def exchange(copies, axis):
    return lax.all_to_all(copies, axis, 0, 0, tiled=True)


def body(features, weights, geno_live, image_live):
    row_count = features.shape[0]
    own_block = features[:, 0, :]
    current = weights[0]
    width = current.shape[1]
    size = window(width)
    dom = ("far", "near")
    doms = lax.axis_size(dom)
    far = lax.axis_size("far")
    feats = lax.axis_size("feat")
    participants = row_count * doms
    step_size = step_rate * participants ** (-0.5)

    joined_size = base_of(far - 1, width) + size
    pad = pltpu.VMEM((K, size), F32)
    line = ((far, K, size), BF16)
    plane = ((NEAR, K, joined_size), BF16)
    rows = ((K, row_count), F32)
    (copies,) = call(
        first_kernel,
        [line],
        [pad],
        [SMEM, SMEM, VMEM],
        geno_live,
        image_live,
        current,
        grant=LARGE,
    )
    for sweep in range(ITERS):
        windows = exchange(copies, "far")
        (copies,) = call(functools.partial(join_kernel, width), [plane], [], [VMEM], windows)
        joined = exchange(copies, "near")
        (copies,) = call(
            functools.partial(project_kernel, far),
            [((feats, K, row_count), F32)],
            [pltpu.VMEM((K, own_block.shape[1]), BF16)],
            [VMEM, VMEM],
            joined,
            own_block,
        )
        partials = exchange(copies, "feat")
        own, partner, copies = call(
            gram_kernel, [rows, rows, ((doms, 8, LANES), F32)], [], [VMEM], partials
        )
        grams = exchange(copies, dom)
        (copies,) = call(
            functools.partial(residual_kernel, participants, far),
            [plane],
            [pltpu.VMEM((K, joined_size), F32)],
            [VMEM] * 4,
            grams,
            own,
            partner,
            own_block,
        )
        joined = exchange(copies, "near")
        (copies,) = call(functools.partial(fold_kernel, width), [line], [], [VMEM], joined)
        shares = exchange(copies, "far")
        operands = (geno_live, image_live, shares, current)
        specs = [SMEM, SMEM, VMEM, VMEM]
        if sweep < ITERS - 1:
            kernel = functools.partial(update_kernel, step_size)
            current, copies = call(kernel, [(current.shape, F32), line], [pad], specs, *operands)
        else:
            kernel = functools.partial(last_kernel, step_size)
            (current,) = call(kernel, [(current.shape, F32)], [], specs, *operands)
    return current[None]


def solution(mesh):
    shape = (mesh.shape["dom"] // NEAR, NEAR, mesh.shape["feat"])
    split = Mesh(mesh.devices.reshape(shape), ("far", "near", "feat"))
    dom = ("far", "near")
    placed = (P(dom, "feat", None), P("feat", None, dom), P(), P())
    return jax.shard_map(
        body, mesh=split, in_specs=placed, out_specs=P("feat", None, dom), check_vma=False
    )
```

```python
import functools
import jax
import jax.numpy as jnp
from jax import lax
from jax.experimental import pallas as pl
from jax.experimental.pallas import tpu as pltpu
from jax.sharding import Mesh
from jax.sharding import PartitionSpec as P

GX = 100000
GY = 50000
K = 32
ITERS = 2
LANES = 128
STEPS = ((1, 0), (0, 1), (1, 1))
HERE = (0, 0)
FAR = ("za", "ya")
DOM = ("za", "zb", "ya", "yb")
AXES = DOM + ("feat",)
CHUNKS = 8
step_rate = 0.1
jitter = 1e-05

VMEM = pl.BlockSpec(memory_space=pltpu.VMEM)
SMEM = pl.BlockSpec(memory_space=pltpu.SMEM)
SMALL = 24 * 1024 * 1024
MEDIUM = 36 * 1024 * 1024
LARGE = 60 * 1024 * 1024
HIGH = lax.Precision.HIGHEST
F32 = jnp.float32
BF16 = jnp.bfloat16


def padded(width):
    return -(-width // LANES) * LANES


def window(width):
    return padded(width + LANES - 16)


def base_of(index, width):
    return (index * width) // LANES * LANES


def offset_of(index, width):
    return lax.rem(index * width, LANES)


def moved(values, source, target, width):
    size = values.shape[1]
    lane = lax.broadcasted_iota(jnp.int32, values.shape, 1)
    values = jnp.where((lane >= source) & (lane < source + width), values, 0.0)
    return pltpu.roll(values, lax.rem(target - source + size, size), 1)


def far_index():
    return lax.axis_index("za") * lax.axis_size("ya") + lax.axis_index("ya")


def shard_index(part, step):
    ya = lax.axis_size("ya")
    z = part // ya * 2 + lax.rem(lax.axis_index("zb") + step[0], 2)
    y = part % ya * 2 + lax.rem(lax.axis_index("yb") + step[1], 2)
    return z * (2 * ya) + y


def route(step, zs, ys, feats):
    def partner(place, size, odd, flip):
        return (place + (1 if place % 2 == odd else -1)) % size if flip else place

    pairs = []
    for z in range(zs):
        for y in range(ys):
            for feat in range(feats):
                odd = feat % 2
                to_z = partner(z, zs, odd, step[0])
                to_y = partner(y, ys, odd, step[1])
                pairs.append(((z * ys + y) * feats + feat, (to_z * ys + to_y) * feats + feat))
    return pairs


def send(message, step):
    zs, ys = 2 * lax.axis_size("za"), 2 * lax.axis_size("ya")
    return lax.ppermute(message, AXES, route(step, zs, ys, lax.axis_size("feat")))


def columns_of(part, step, width):
    begin = shard_index(part, step) * width
    base = pl.multiple_of(lax.div(begin, LANES) * LANES, LANES)
    return pl.ds(base, window(width)), lax.rem(begin, LANES)


def is_geno():
    return lax.axis_index("feat") < lax.axis_size("feat") // 2


def lane_mask(geno_live, image_live, width):
    slot = lax.rem(lax.axis_index("feat"), lax.axis_size("feat") // 2)
    live = jnp.where(is_geno(), geno_live[slot], image_live[slot])
    shard = lax.axis_index(DOM)
    column = lax.broadcasted_iota(jnp.int32, (K, width), 1) + shard * width
    return (column < live).astype(F32)


def spread(masked, width, pad, copies):
    pad[...] = jnp.zeros(pad.shape, F32)
    pad[:, :width] = masked
    shift = offset_of(far_index(), width)
    rounded = pltpu.roll(pad[...], shift, 1).astype(BF16)
    for copy in range(copies.shape[0]):
        copies[copy] = rounded


def first_kernel(geno_live, image_live, weights, copies, pad):
    width = weights.shape[1]
    masked = weights[...] * lane_mask(geno_live, image_live, width)
    spread(masked, width, pad, copies)


def join_kernel(width, windows, joined):
    size = windows.shape[2]
    joined[...] = jnp.zeros(joined.shape, BF16)
    for part in range(windows.shape[0]):
        base = base_of(part, width)
        joined[:, base : base + size] += windows[part]


def projected(far, steps, pieces, features, total):
    width = features.shape[1] // (far * 4)
    size = window(width)
    for step, piece in zip(steps, pieces):
        for part in range(far):
            columns, begin = columns_of(part, step, width)
            start = base_of(part, width)
            weights = piece[:, start : start + size].astype(F32)
            weights = moved(weights, part * width % LANES, begin, width).astype(BF16)
            product = lax.dot_general(
                features[:, columns],
                weights,
                (((1,), (1,)), ((), ())),
                preferred_element_type=F32,
            )
            total = product if total is None else total + product
    return total


def project_first_kernel(far, features, joined, total, held, arrived):
    rows = features.shape[0] // CHUNKS
    copies = []
    for chunk in range(CHUNKS):
        place = pl.ds(chunk * rows, rows)
        copies.append(
            pltpu.make_async_copy(features.at[place], held.at[place], arrived.at[chunk])
        )
        copies[-1].start()
    for copy in copies:
        copy.wait()
    total[...] = projected(far, (HERE,), (joined,), held, None)


def project_own_kernel(far, steps, features, *rest):
    *pieces, total = rest
    total[...] = projected(far, steps, pieces, features, None)


def project_kernel(far, steps, features, before, *rest):
    *pieces, total = rest
    total[...] = projected(far, steps, pieces, features, before[...])


def project_last_kernel(far, steps, features, before, *rest):
    *pieces, copies = rest
    total = projected(far, steps, pieces, features, before[...]).T
    for copy in range(copies.shape[0]):
        copies[copy] = total


def gram_kernel(partials, own, partner, copies):
    half = partials.shape[0] // 2
    geno = partials[0]
    image = partials[half]
    for block in range(1, half):
        geno += partials[block]
        image += partials[half + block]
    geno *= GX ** (-0.5)
    image *= GY ** (-0.5)
    own[...] = jnp.where(is_geno(), geno, image)
    other = jnp.where(is_geno(), image, geno)
    partner[...] = other
    tiled = jnp.concatenate([other] * (LANES // K), axis=0)
    gram = lax.dot_general(
        other, tiled, (((1,), (1,)), ((), ())), precision=HIGH, preferred_element_type=F32
    )
    lane = lax.broadcasted_iota(jnp.int32, (8, LANES), 1)
    packed = jnp.zeros((8, LANES), F32)
    for part in range(LANES // K):
        packed = jnp.where(lane // K == part, gram[8 * part : 8 * part + 8], packed)
    for copy in range(copies.shape[0]):
        copies[copy] = packed


def residual_kernel(participants, grams, own, partner, residual):
    total = grams[0]
    for part in range(1, grams.shape[0]):
        total += grams[part]
    rows = [total] + [pltpu.roll(total, LANES - K * part, 1) for part in range(1, LANES // K)]
    row = lax.broadcasted_iota(jnp.int32, (K, LANES), 0)
    lane = lax.broadcasted_iota(jnp.int32, (K, LANES), 1)
    covariance = jnp.concatenate(rows, axis=0) / participants
    covariance += jnp.where(lane == row, jitter, 0.0)
    state = jnp.where(lane < K, covariance, jnp.where(lane == row + K, 1.0, 0.0))
    pivots = jnp.zeros((K, 1), F32)
    for step in range(K):
        pivot_row = state[step : step + 1, :]
        column = state[:, step : step + 1]
        pivot = pivot_row[:, step : step + 1]
        pivots = jnp.where(row[:, :1] == step, pivot, pivots)
        ratio = jnp.where(row[:, :1] > step, column / pivot, 0.0)
        state = state - ratio * pivot_row
    scaled = state * lax.rsqrt(pivots)
    inverse = pltpu.roll(scaled, LANES - K, 1)[:, :K]
    target = lax.dot_general(
        inverse, partner[...], (((1,), (0,)), ((), ())), precision=HIGH, preferred_element_type=F32
    )
    residual[...] = (own[...] - target).astype(BF16)


def message_row(far, step, residual, features, row):
    width = features.shape[1] // (far * 4)
    size = window(width)
    row[...] = jnp.zeros(row.shape, F32)
    for part in range(far):
        columns, begin = columns_of(part, step, width)
        piece = lax.dot_general(
            residual[...],
            features[:, columns],
            (((1,), (0,)), ((), ())),
            preferred_element_type=F32,
        )
        start = base_of(part, width)
        row[:, start : start + size] += moved(piece, begin, part * width % LANES, width)


def message_kernel(far, steps, residual, features, *rest):
    *messages, row = rest
    for step, message in zip(steps, messages):
        message_row(far, step, residual, features, row)
        message[...] = row[...].astype(BF16)


def kept_kernel(far, residual, features, received, kept):
    message_row(far, HERE, residual, features, kept)
    kept[...] += received[...].astype(F32)


def fold_kernel(width, own, *rest):
    *received, windows = rest
    total = own[...]
    for message in received:
        total += message[...].astype(F32)
    total = total.astype(BF16)
    size = windows.shape[2]
    for part in range(windows.shape[0]):
        start = base_of(part, width)
        windows[part] = total[:, start : start + size]


def updated_weights(step_size, geno_live, image_live, windows, weights):
    width = weights.shape[1]
    total = windows[0].astype(F32)
    for part in range(1, windows.shape[0]):
        total += windows[part].astype(F32)
    size = windows.shape[2]
    shift = lax.rem(size - offset_of(far_index(), width), size)
    gradient = pltpu.roll(total, shift, 1)[:, :width]
    return lane_mask(geno_live, image_live, width) * (weights[...] - step_size * gradient)


def update_kernel(step_size, geno_live, image_live, windows, weights, updated, copies, pad):
    fresh = updated_weights(step_size, geno_live, image_live, windows, weights)
    updated[...] = fresh
    spread(fresh, weights.shape[1], pad, copies)


def last_kernel(step_size, geno_live, image_live, windows, weights, updated):
    updated[...] = updated_weights(step_size, geno_live, image_live, windows, weights)


def call(kernel, outs, scratch, specs, *operands, grant=SMALL, flops=0):
    shapes = tuple(jax.ShapeDtypeStruct(*out) for out in outs)
    return pl.pallas_call(
        kernel,
        out_shape=shapes,
        in_specs=specs,
        out_specs=tuple(VMEM for _ in shapes),
        scratch_shapes=list(scratch),
        compiler_params=pltpu.CompilerParams(vmem_limit_bytes=grant),
        cost_estimate=pl.CostEstimate(flops=flops, bytes_accessed=1 << 10, transcendentals=0),
    )(*operands)


def exchange(copies, axis):
    return lax.all_to_all(copies, axis, 0, 0, tiled=True)


def body(features, weights, geno_live, image_live):
    row_count = features.shape[0]
    own_block = features[:, 0, :]
    current = weights[0]
    width = current.shape[1]
    size = window(width)
    doms = lax.axis_size(DOM)
    far = lax.axis_size(FAR)
    feats = lax.axis_size("feat")
    participants = row_count * doms
    step_size = step_rate * participants ** (-0.5)

    joined_size = base_of(far - 1, width) + size
    pad = pltpu.VMEM((K, size), F32)
    line = ((far, K, size), BF16)
    message = (K, joined_size)
    rows = ((K, row_count), F32)
    total = ((row_count, K), F32)
    partial = ((feats, K, row_count), F32)
    piece_flops = 2 * row_count * K * joined_size

    def project(kernel, out, steps, *operands):
        kernel = functools.partial(kernel, far, steps)
        flops = piece_flops * len(steps)
        return call(kernel, [out], [], [VMEM] * len(operands), *operands, flops=flops)[0]

    def messages(residual, held, steps):
        return call(
            functools.partial(message_kernel, far, steps),
            [(message, BF16)] * len(steps),
            [pltpu.VMEM(message, F32)],
            [VMEM, VMEM],
            residual,
            held,
        )

    (copies,) = call(
        first_kernel,
        [line],
        [pad],
        [SMEM, SMEM, VMEM],
        geno_live,
        image_live,
        current,
        grant=LARGE,
    )
    for sweep in range(ITERS):
        windows = exchange(copies, FAR)
        (joined,) = call(
            functools.partial(join_kernel, width), [(message, BF16)], [], [VMEM], windows
        )
        received = [send(joined, step) for step in STEPS]
        if sweep == 0:
            part, held = call(
                functools.partial(project_first_kernel, far),
                [total, (own_block.shape, BF16)],
                [pltpu.SemaphoreType.DMA((CHUNKS,))],
                [pl.BlockSpec(memory_space=pl.ANY), VMEM],
                own_block,
                joined,
                grant=MEDIUM,
                flops=piece_flops,
            )
        else:
            part = project(project_own_kernel, total, (HERE,), held, joined)
        part = project(project_kernel, total, STEPS[:2], held, part, *received[:2])
        copies = project(project_last_kernel, partial, STEPS[2:], held, part, *received[2:])
        partials = exchange(copies, "feat")
        own, partner, copies = call(
            gram_kernel, [rows, rows, ((doms, 8, LANES), F32)], [], [VMEM], partials
        )
        grams = exchange(copies, DOM)
        (residual,) = call(
            functools.partial(residual_kernel, participants),
            [((K, row_count), BF16)],
            [],
            [VMEM] * 3,
            grams,
            own,
            partner,
        )
        (made,) = messages(residual, held, STEPS[2:])
        first = send(made, STEPS[2])
        made = messages(residual, held, STEPS[:2])
        received = [send(item, step) for item, step in zip(made, STEPS[:2])]
        kernel = functools.partial(kept_kernel, far)
        (kept,) = call(kernel, [(message, F32)], [], [VMEM] * 3, residual, held, first)
        kernel = functools.partial(fold_kernel, width)
        (copies,) = call(kernel, [line], [], [VMEM] * 3, kept, *received)
        shares = exchange(copies, FAR)
        operands = (geno_live, image_live, shares, current)
        specs = [SMEM, SMEM, VMEM, VMEM]
        if sweep < ITERS - 1:
            kernel = functools.partial(update_kernel, step_size)
            current, copies = call(kernel, [(current.shape, F32), line], [pad], specs, *operands)
        else:
            kernel = functools.partial(last_kernel, step_size)
            (current,) = call(kernel, [(current.shape, F32)], [], specs, *operands)
    return current[None]


def solution(mesh):
    ys = 4
    shape = (mesh.shape["dom"] // ys // 2, 2, ys // 2, 2, mesh.shape["feat"])
    split = Mesh(mesh.devices.reshape(shape), AXES)
    placed = (P(DOM, "feat", None), P("feat", None, DOM), P(), P())
    return jax.shard_map(
        body, mesh=split, in_specs=placed, out_specs=P("feat", None, DOM), check_vma=False
    )
```

```python
import functools
import jax
import jax.numpy as jnp
from jax import lax
from jax.experimental import pallas as pl
from jax.experimental.pallas import tpu as pltpu
from jax.sharding import Mesh
from jax.sharding import PartitionSpec as P

GX = 100000
GY = 50000
K = 32
ITERS = 2
LANES = 128
STEPS = ((1, 0), (0, 1), (1, 1))
HERE = (0, 0)
FAR = ("za", "ya")
DOM = ("za", "zb", "ya", "yb")
AXES = DOM + ("feat",)
CHUNKS = 8
step_rate = 0.1
jitter = 1e-05

VMEM = pl.BlockSpec(memory_space=pltpu.VMEM)
SMEM = pl.BlockSpec(memory_space=pltpu.SMEM)
SMALL = 24 * 1024 * 1024
MEDIUM = 36 * 1024 * 1024
LARGE = 60 * 1024 * 1024
HIGH = lax.Precision.HIGHEST
F32 = jnp.float32
BF16 = jnp.bfloat16


def padded(width):
    return -(-width // LANES) * LANES


def window(width):
    return padded(width + LANES - 16)


def base_of(index, width):
    return (index * width) // LANES * LANES


def offset_of(index, width):
    return lax.rem(index * width, LANES)


def moved(values, source, target, width):
    size = values.shape[1]
    lane = lax.broadcasted_iota(jnp.int32, values.shape, 1)
    values = jnp.where((lane >= source) & (lane < source + width), values, 0.0)
    return pltpu.roll(values, lax.rem(target - source + size, size), 1)


def far_index():
    return lax.axis_index("za") * lax.axis_size("ya") + lax.axis_index("ya")


def shard_index(part, step):
    ya = lax.axis_size("ya")
    z = part // ya * 2 + lax.rem(lax.axis_index("zb") + step[0], 2)
    y = part % ya * 2 + lax.rem(lax.axis_index("yb") + step[1], 2)
    return z * (2 * ya) + y


def route(step, zs, ys, feats):
    def partner(place, size, odd, flip):
        return (place + (1 if place % 2 == odd else -1)) % size if flip else place

    pairs = []
    for z in range(zs):
        for y in range(ys):
            for feat in range(feats):
                odd = feat % 2
                to_z = partner(z, zs, odd, step[0])
                to_y = partner(y, ys, odd, step[1])
                pairs.append(((z * ys + y) * feats + feat, (to_z * ys + to_y) * feats + feat))
    return pairs


def send(message, step):
    zs, ys = 2 * lax.axis_size("za"), 2 * lax.axis_size("ya")
    return lax.ppermute(message, AXES, route(step, zs, ys, lax.axis_size("feat")))


def columns_of(part, step, width):
    begin = shard_index(part, step) * width
    base = pl.multiple_of(lax.div(begin, LANES) * LANES, LANES)
    return pl.ds(base, window(width)), lax.rem(begin, LANES)


def is_geno():
    return lax.axis_index("feat") < lax.axis_size("feat") // 2


def lane_mask(geno_live, image_live, width):
    slot = lax.rem(lax.axis_index("feat"), lax.axis_size("feat") // 2)
    live = jnp.where(is_geno(), geno_live[slot], image_live[slot])
    shard = lax.axis_index(DOM)
    column = lax.broadcasted_iota(jnp.int32, (K, width), 1) + shard * width
    return (column < live).astype(F32)


def spread(masked, width, pad, copies):
    pad[...] = jnp.zeros(pad.shape, F32)
    pad[:, :width] = masked
    shift = offset_of(far_index(), width)
    rounded = pltpu.roll(pad[...], shift, 1).astype(BF16)
    for copy in range(copies.shape[0]):
        copies[copy] = rounded


def first_kernel(geno_live, image_live, weights, copies, pad):
    width = weights.shape[1]
    masked = weights[...] * lane_mask(geno_live, image_live, width)
    spread(masked, width, pad, copies)


def join_kernel(width, windows, joined):
    size = windows.shape[2]
    joined[...] = jnp.zeros(joined.shape, BF16)
    for part in range(windows.shape[0]):
        base = base_of(part, width)
        joined[:, base : base + size] += windows[part]


def projected(far, steps, pieces, features, total):
    width = features.shape[1] // (far * 4)
    size = window(width)
    for step, piece in zip(steps, pieces):
        for part in range(far):
            columns, begin = columns_of(part, step, width)
            start = base_of(part, width)
            weights = piece[:, start : start + size].astype(F32)
            weights = moved(weights, part * width % LANES, begin, width).astype(BF16)
            product = lax.dot_general(
                features[:, columns],
                weights,
                (((1,), (1,)), ((), ())),
                preferred_element_type=F32,
            )
            total = product if total is None else total + product
    return total


def project_first_kernel(far, features, joined, total, held, arrived):
    rows = features.shape[0] // CHUNKS
    copies = []
    for chunk in range(CHUNKS):
        place = pl.ds(chunk * rows, rows)
        copies.append(
            pltpu.make_async_copy(features.at[place], held.at[place], arrived.at[chunk])
        )
        copies[-1].start()
    for copy in copies:
        copy.wait()
    total[...] = projected(far, (HERE,), (joined,), held, None)


def project_own_kernel(far, steps, features, *rest):
    *pieces, total = rest
    total[...] = projected(far, steps, pieces, features, None)


def project_kernel(far, steps, features, before, *rest):
    *pieces, total = rest
    total[...] = projected(far, steps, pieces, features, before[...])


def project_last_kernel(far, steps, features, before, *rest):
    *pieces, copies = rest
    total = projected(far, steps, pieces, features, before[...]).T
    for copy in range(copies.shape[0]):
        copies[copy] = total


def gram_kernel(partials, own, partner, copies):
    half = partials.shape[0] // 2
    geno = partials[0]
    image = partials[half]
    for block in range(1, half):
        geno += partials[block]
        image += partials[half + block]
    geno *= GX ** (-0.5)
    image *= GY ** (-0.5)
    own[...] = jnp.where(is_geno(), geno, image)
    other = jnp.where(is_geno(), image, geno)
    partner[...] = other
    tiled = jnp.concatenate([other] * (LANES // K), axis=0)
    gram = lax.dot_general(
        other, tiled, (((1,), (1,)), ((), ())), precision=HIGH, preferred_element_type=F32
    )
    lane = lax.broadcasted_iota(jnp.int32, (8, LANES), 1)
    packed = jnp.zeros((8, LANES), F32)
    for part in range(LANES // K):
        packed = jnp.where(lane // K == part, gram[8 * part : 8 * part + 8], packed)
    for copy in range(copies.shape[0]):
        copies[copy] = packed


def message_row(far, step, residual, features, row):
    width = features.shape[1] // (far * 4)
    size = window(width)
    row[...] = jnp.zeros(row.shape, F32)
    for part in range(far):
        columns, begin = columns_of(part, step, width)
        piece = lax.dot_general(
            residual[...],
            features[:, columns],
            (((1,), (0,)), ((), ())),
            preferred_element_type=F32,
        )
        start = base_of(part, width)
        row[:, start : start + size] += moved(piece, begin, part * width % LANES, width)


def residual_kernel(participants, far, grams, own, partner, features, residual, message, row_sum):
    total = grams[0]
    for part in range(1, grams.shape[0]):
        total += grams[part]
    rows = [total] + [pltpu.roll(total, LANES - K * part, 1) for part in range(1, LANES // K)]
    row = lax.broadcasted_iota(jnp.int32, (K, LANES), 0)
    lane = lax.broadcasted_iota(jnp.int32, (K, LANES), 1)
    covariance = jnp.concatenate(rows, axis=0) / participants
    covariance += jnp.where(lane == row, jitter, 0.0)
    state = jnp.where(lane < K, covariance, jnp.where(lane == row + K, 1.0, 0.0))
    for step in range(K):
        column = jnp.broadcast_to(state[:, step : step + 1], state.shape)
        scaled_row = state[step : step + 1, :] / column[step : step + 1, :]
        state = state - jnp.where(row > step, column, 0.0) * scaled_row
    pivots = jnp.sum(jnp.where(lane == row, state, 0.0), axis=1, keepdims=True)
    scaled = state * lax.rsqrt(pivots)
    inverse = pltpu.roll(scaled, LANES - K, 1)[:, :K]
    target = lax.dot_general(
        inverse, partner[...], (((1,), (0,)), ((), ())), precision=HIGH, preferred_element_type=F32
    )
    residual[...] = (own[...] - target).astype(BF16)
    message_row(far, STEPS[2], residual, features, row_sum)
    message[...] = row_sum[...].astype(BF16)


def message_kernel(far, steps, residual, features, *rest):
    *messages, row = rest
    for step, message in zip(steps, messages):
        message_row(far, step, residual, features, row)
        message[...] = row[...].astype(BF16)


def kept_kernel(far, residual, features, received, kept):
    message_row(far, HERE, residual, features, kept)
    kept[...] += received[...].astype(F32)


def fold_kernel(width, own, *rest):
    *received, windows = rest
    total = own[...]
    for message in received:
        total += message[...].astype(F32)
    total = total.astype(BF16)
    size = windows.shape[2]
    for part in range(windows.shape[0]):
        start = base_of(part, width)
        windows[part] = total[:, start : start + size]


def updated_weights(step_size, geno_live, image_live, windows, weights):
    width = weights.shape[1]
    total = windows[0].astype(F32)
    for part in range(1, windows.shape[0]):
        total += windows[part].astype(F32)
    size = windows.shape[2]
    shift = lax.rem(size - offset_of(far_index(), width), size)
    gradient = pltpu.roll(total, shift, 1)[:, :width]
    return lane_mask(geno_live, image_live, width) * (weights[...] - step_size * gradient)


def update_kernel(step_size, geno_live, image_live, windows, weights, updated, copies, pad):
    fresh = updated_weights(step_size, geno_live, image_live, windows, weights)
    updated[...] = fresh
    spread(fresh, weights.shape[1], pad, copies)


def last_kernel(step_size, geno_live, image_live, windows, weights, updated):
    updated[...] = updated_weights(step_size, geno_live, image_live, windows, weights)


def call(kernel, outs, scratch, specs, *operands, grant=SMALL, flops=0):
    shapes = tuple(jax.ShapeDtypeStruct(*out) for out in outs)
    return pl.pallas_call(
        kernel,
        out_shape=shapes,
        in_specs=specs,
        out_specs=tuple(VMEM for _ in shapes),
        scratch_shapes=list(scratch),
        compiler_params=pltpu.CompilerParams(vmem_limit_bytes=grant),
        cost_estimate=pl.CostEstimate(flops=flops, bytes_accessed=1 << 10, transcendentals=0),
    )(*operands)


def exchange(copies, axis):
    return lax.all_to_all(copies, axis, 0, 0, tiled=True)


def body(features, weights, geno_live, image_live):
    row_count = features.shape[0]
    own_block = features[:, 0, :]
    current = weights[0]
    width = current.shape[1]
    size = window(width)
    doms = lax.axis_size(DOM)
    far = lax.axis_size(FAR)
    feats = lax.axis_size("feat")
    participants = row_count * doms
    step_size = step_rate * participants ** (-0.5)

    joined_size = base_of(far - 1, width) + size
    pad = pltpu.VMEM((K, size), F32)
    line = ((far, K, size), BF16)
    message = ((K, joined_size), BF16)
    rows = ((K, row_count), F32)
    total = ((row_count, K), F32)
    partial = ((feats, K, row_count), F32)
    piece_flops = 2 * row_count * K * joined_size

    def project(kernel, out, steps, *operands):
        kernel = functools.partial(kernel, far, steps)
        flops = piece_flops * len(steps)
        return call(kernel, [out], [], [VMEM] * len(operands), *operands, flops=flops)[0]

    def messages(residual, held, steps):
        return call(
            functools.partial(message_kernel, far, steps),
            [message] * len(steps),
            [pltpu.VMEM(message[0], F32)],
            [VMEM, VMEM],
            residual,
            held,
            flops=piece_flops * len(steps) * 8,
        )

    (copies,) = call(
        first_kernel,
        [line],
        [pad],
        [SMEM, SMEM, VMEM],
        geno_live,
        image_live,
        current,
        grant=LARGE,
    )
    for sweep in range(ITERS):
        windows = exchange(copies, FAR)
        (joined,) = call(
            functools.partial(join_kernel, width), [message], [], [VMEM], windows
        )
        received = [send(joined, step) for step in STEPS]
        if sweep == 0:
            part, held = call(
                functools.partial(project_first_kernel, far),
                [total, (own_block.shape, BF16)],
                [pltpu.SemaphoreType.DMA((CHUNKS,))],
                [pl.BlockSpec(memory_space=pl.ANY), VMEM],
                own_block,
                joined,
                grant=MEDIUM,
                flops=piece_flops,
            )
        else:
            part = project(project_own_kernel, total, (HERE,), held, joined)
        part = project(project_kernel, total, STEPS[:2], held, part, *received[:2])
        copies = project(project_last_kernel, partial, STEPS[2:], held, part, *received[2:])
        partials = exchange(copies, "feat")
        own, partner, copies = call(
            gram_kernel, [rows, rows, ((doms, 8, LANES), F32)], [], [VMEM], partials
        )
        grams = exchange(copies, DOM)
        residual, made = call(
            functools.partial(residual_kernel, participants, far),
            [((K, row_count), BF16), message],
            [pltpu.VMEM(message[0], F32)],
            [VMEM] * 4,
            grams,
            own,
            partner,
            held,
        )
        first = send(made, STEPS[2])
        made = messages(residual, held, STEPS[:2])
        received = [send(item, step) for item, step in zip(made, STEPS[:2])]
        kernel = functools.partial(kept_kernel, far)
        (kept,) = call(
            kernel, [(message[0], F32)], [], [VMEM] * 3, residual, held, first, flops=piece_flops * 8
        )
        kernel = functools.partial(fold_kernel, width)
        (copies,) = call(kernel, [line], [], [VMEM] * 3, kept, *received)
        shares = exchange(copies, FAR)
        operands = (geno_live, image_live, shares, current)
        specs = [SMEM, SMEM, VMEM, VMEM]
        if sweep < ITERS - 1:
            kernel = functools.partial(update_kernel, step_size)
            current, copies = call(kernel, [(current.shape, F32), line], [pad], specs, *operands)
        else:
            kernel = functools.partial(last_kernel, step_size)
            (current,) = call(kernel, [(current.shape, F32)], [], specs, *operands)
    return current[None]


def solution(mesh):
    ys = 4
    shape = (mesh.shape["dom"] // ys // 2, 2, ys // 2, 2, mesh.shape["feat"])
    split = Mesh(mesh.devices.reshape(shape), AXES)
    placed = (P(DOM, "feat", None), P("feat", None, DOM), P(), P())
    return jax.shard_map(
        body, mesh=split, in_specs=placed, out_specs=P("feat", None, DOM), check_vma=False
    )
```

```python
import functools
import jax
import jax.numpy as jnp
from jax import lax
from jax.experimental import pallas as pl
from jax.experimental.pallas import tpu as pltpu
from jax.sharding import Mesh
from jax.sharding import PartitionSpec as P

GX = 100000
GY = 50000
K = 32
ITERS = 2
LANES = 128
STEPS = ((1, 0), (0, 1), (1, 1))
HERE = (0, 0)
FAR = ("za", "ya")
DOM = ("za", "zb", "ya", "yb")
AXES = DOM + ("feat",)
CHUNKS = 8
GROUP = 8
step_rate = 0.1
jitter = 1e-05

VMEM = pl.BlockSpec(memory_space=pltpu.VMEM)
SMEM = pl.BlockSpec(memory_space=pltpu.SMEM)
SMALL = 24 * 1024 * 1024
MEDIUM = 36 * 1024 * 1024
LARGE = 60 * 1024 * 1024
HIGH = lax.Precision.HIGHEST
F32 = jnp.float32
BF16 = jnp.bfloat16


def padded(width):
    return -(-width // LANES) * LANES


def window(width):
    return padded(width + LANES - 16)


def base_of(index, width):
    return (index * width) // LANES * LANES


def offset_of(index, width):
    return lax.rem(index * width, LANES)


def moved(values, source, target, width):
    size = values.shape[1]
    lane = lax.broadcasted_iota(jnp.int32, values.shape, 1)
    values = jnp.where((lane >= source) & (lane < source + width), values, 0.0)
    return pltpu.roll(values, lax.rem(target - source + size, size), 1)


def far_index():
    return lax.axis_index("za") * lax.axis_size("ya") + lax.axis_index("ya")


def shard_index(part, step):
    ya = lax.axis_size("ya")
    z = part // ya * 2 + lax.rem(lax.axis_index("zb") + step[0], 2)
    y = part % ya * 2 + lax.rem(lax.axis_index("yb") + step[1], 2)
    return z * (2 * ya) + y


def route(step, zs, ys, feats):
    def partner(place, size, odd, flip):
        return (place + (1 if place % 2 == odd else -1)) % size if flip else place

    pairs = []
    for z in range(zs):
        for y in range(ys):
            for feat in range(feats):
                odd = feat % 2
                to_z = partner(z, zs, odd, step[0])
                to_y = partner(y, ys, odd, step[1])
                pairs.append(((z * ys + y) * feats + feat, (to_z * ys + to_y) * feats + feat))
    return pairs


def send(message, step):
    zs, ys = 2 * lax.axis_size("za"), 2 * lax.axis_size("ya")
    return lax.ppermute(message, AXES, route(step, zs, ys, lax.axis_size("feat")))


def columns_of(part, step, width):
    begin = shard_index(part, step) * width
    base = pl.multiple_of(lax.div(begin, LANES) * LANES, LANES)
    return pl.ds(base, window(width)), lax.rem(begin, LANES)


def is_geno():
    return lax.axis_index("feat") < lax.axis_size("feat") // 2


def lane_mask(geno_live, image_live, width):
    slot = lax.rem(lax.axis_index("feat"), lax.axis_size("feat") // 2)
    live = jnp.where(is_geno(), geno_live[slot], image_live[slot])
    shard = lax.axis_index(DOM)
    column = lax.broadcasted_iota(jnp.int32, (K, width), 1) + shard * width
    return (column < live).astype(F32)


def spread(masked, width, pad, copies):
    pad[...] = jnp.zeros(pad.shape, F32)
    pad[:, :width] = masked
    shift = offset_of(far_index(), width)
    rounded = pltpu.roll(pad[...], shift, 1).astype(BF16)
    for copy in range(copies.shape[0]):
        copies[copy] = rounded


def first_kernel(geno_live, image_live, weights, copies, pad):
    width = weights.shape[1]
    masked = weights[...] * lane_mask(geno_live, image_live, width)
    spread(masked, width, pad, copies)


def join_kernel(width, windows, joined):
    size = windows.shape[2]
    joined[...] = jnp.zeros(joined.shape, BF16)
    for part in range(windows.shape[0]):
        base = base_of(part, width)
        joined[:, base : base + size] += windows[part]


def projected(far, steps, pieces, features, total):
    width = features.shape[1] // (far * 4)
    size = window(width)
    for step, piece in zip(steps, pieces):
        for part in range(far):
            columns, begin = columns_of(part, step, width)
            start = base_of(part, width)
            weights = piece[:, start : start + size].astype(F32)
            weights = moved(weights, part * width % LANES, begin, width).astype(BF16)
            product = lax.dot_general(
                features[:, columns],
                weights,
                (((1,), (1,)), ((), ())),
                preferred_element_type=F32,
            )
            total = product if total is None else total + product
    return total


def project_first_kernel(far, features, joined, total, held, arrived):
    rows = features.shape[0] // CHUNKS
    copies = []
    for chunk in range(CHUNKS):
        place = pl.ds(chunk * rows, rows)
        copies.append(
            pltpu.make_async_copy(features.at[place], held.at[place], arrived.at[chunk])
        )
        copies[-1].start()
    for copy in copies:
        copy.wait()
    total[...] = projected(far, (HERE,), (joined,), held, None)


def project_own_kernel(far, steps, features, *rest):
    *pieces, total = rest
    total[...] = projected(far, steps, pieces, features, None)


def project_kernel(far, steps, features, before, *rest):
    *pieces, total = rest
    total[...] = projected(far, steps, pieces, features, before[...])


def project_last_kernel(far, steps, features, before, *rest):
    *pieces, copies = rest
    total = projected(far, steps, pieces, features, before[...]).T
    for copy in range(copies.shape[0]):
        copies[copy] = total


def gram_kernel(partials, own, partner, copies):
    half = partials.shape[0] // 2
    geno = partials[0]
    image = partials[half]
    for block in range(1, half):
        geno += partials[block]
        image += partials[half + block]
    geno *= GX ** (-0.5)
    image *= GY ** (-0.5)
    own[...] = jnp.where(is_geno(), geno, image)
    other = jnp.where(is_geno(), image, geno)
    partner[...] = other
    tiled = jnp.concatenate([other] * (LANES // K), axis=0)
    gram = lax.dot_general(
        other, tiled, (((1,), (1,)), ((), ())), precision=HIGH, preferred_element_type=F32
    )
    lane = lax.broadcasted_iota(jnp.int32, (8, LANES), 1)
    packed = jnp.zeros((8, LANES), F32)
    for part in range(LANES // K):
        packed = jnp.where(lane // K == part, gram[8 * part : 8 * part + 8], packed)
    for copy in range(copies.shape[0]):
        copies[copy] = packed


def message_row(far, step, residual, features, row):
    width = features.shape[1] // (far * 4)
    size = window(width)
    row[...] = jnp.zeros(row.shape, F32)
    for part in range(far):
        columns, begin = columns_of(part, step, width)
        piece = lax.dot_general(
            residual[...],
            features[:, columns],
            (((1,), (0,)), ((), ())),
            preferred_element_type=F32,
        )
        start = base_of(part, width)
        row[:, start : start + size] += moved(piece, begin, part * width % LANES, width)


def residual_kernel(participants, far, grams, own, partner, features, residual, message, row_sum):
    total = grams[0]
    for part in range(1, grams.shape[0]):
        total += grams[part]
    rows = [total] + [pltpu.roll(total, LANES - K * part, 1) for part in range(1, LANES // K)]
    row = lax.broadcasted_iota(jnp.int32, (K, LANES), 0)
    lane = lax.broadcasted_iota(jnp.int32, (K, LANES), 1)
    covariance = jnp.concatenate(rows, axis=0) / participants
    covariance += jnp.where(lane == row, jitter, 0.0)
    state = jnp.where(lane < K, covariance, jnp.where(lane == row + K, 1.0, 0.0))
    for base in range(0, K, GROUP):
        columns = [
            jnp.broadcast_to(state[:, base + i : base + i + 1], state.shape) for i in range(GROUP)
        ]
        rows = [state[base + i : base + i + 1, :] for i in range(GROUP)]
        for i in range(GROUP):
            step = base + i
            inverse = 1.0 / columns[i][step : step + 1, :]
            below = jnp.where(row > step, columns[i], 0.0)
            for later in range(i + 1, GROUP):
                ratio = columns[i][base + later : base + later + 1, :] * inverse
                columns[later] = columns[later] - below * ratio
                rows[later] = rows[later] - rows[i] * ratio
            state = state - below * (rows[i] * inverse)
    pivots = jnp.sum(jnp.where(lane == row, state, 0.0), axis=1, keepdims=True)
    scaled = state * lax.rsqrt(pivots)
    inverse = pltpu.roll(scaled, LANES - K, 1)[:, :K]
    target = lax.dot_general(
        inverse, partner[...], (((1,), (0,)), ((), ())), precision=HIGH, preferred_element_type=F32
    )
    residual[...] = (own[...] - target).astype(BF16)
    message_row(far, STEPS[2], residual, features, row_sum)
    message[...] = row_sum[...].astype(BF16)


def message_kernel(far, steps, residual, features, *rest):
    *messages, row = rest
    for step, message in zip(steps, messages):
        message_row(far, step, residual, features, row)
        message[...] = row[...].astype(BF16)


def kept_kernel(far, residual, features, received, kept):
    message_row(far, HERE, residual, features, kept)
    kept[...] += received[...].astype(F32)


def fold_kernel(width, own, *rest):
    *received, windows = rest
    total = own[...]
    for message in received:
        total += message[...].astype(F32)
    total = total.astype(BF16)
    size = windows.shape[2]
    for part in range(windows.shape[0]):
        start = base_of(part, width)
        windows[part] = total[:, start : start + size]


def updated_weights(step_size, geno_live, image_live, windows, weights):
    width = weights.shape[1]
    total = windows[0].astype(F32)
    for part in range(1, windows.shape[0]):
        total += windows[part].astype(F32)
    size = windows.shape[2]
    shift = lax.rem(size - offset_of(far_index(), width), size)
    gradient = pltpu.roll(total, shift, 1)[:, :width]
    return lane_mask(geno_live, image_live, width) * (weights[...] - step_size * gradient)


def update_kernel(step_size, geno_live, image_live, windows, weights, updated, copies, pad):
    fresh = updated_weights(step_size, geno_live, image_live, windows, weights)
    updated[...] = fresh
    spread(fresh, weights.shape[1], pad, copies)


def last_kernel(step_size, geno_live, image_live, windows, weights, updated):
    updated[...] = updated_weights(step_size, geno_live, image_live, windows, weights)


def call(kernel, outs, scratch, specs, *operands, grant=SMALL, flops=0):
    shapes = tuple(jax.ShapeDtypeStruct(*out) for out in outs)
    return pl.pallas_call(
        kernel,
        out_shape=shapes,
        in_specs=specs,
        out_specs=tuple(VMEM for _ in shapes),
        scratch_shapes=list(scratch),
        compiler_params=pltpu.CompilerParams(vmem_limit_bytes=grant),
        cost_estimate=pl.CostEstimate(flops=flops, bytes_accessed=1 << 10, transcendentals=0),
    )(*operands)


def exchange(copies, axis):
    return lax.all_to_all(copies, axis, 0, 0, tiled=True)


def body(features, weights, geno_live, image_live):
    row_count = features.shape[0]
    own_block = features[:, 0, :]
    current = weights[0]
    width = current.shape[1]
    size = window(width)
    doms = lax.axis_size(DOM)
    far = lax.axis_size(FAR)
    feats = lax.axis_size("feat")
    participants = row_count * doms
    step_size = step_rate * participants ** (-0.5)

    joined_size = base_of(far - 1, width) + size
    pad = pltpu.VMEM((K, size), F32)
    line = ((far, K, size), BF16)
    message = ((K, joined_size), BF16)
    rows = ((K, row_count), F32)
    total = ((row_count, K), F32)
    partial = ((feats, K, row_count), F32)
    piece_flops = 2 * row_count * K * joined_size

    def project(kernel, out, steps, *operands):
        kernel = functools.partial(kernel, far, steps)
        flops = piece_flops * len(steps)
        return call(kernel, [out], [], [VMEM] * len(operands), *operands, flops=flops)[0]

    def messages(residual, held, steps):
        return call(
            functools.partial(message_kernel, far, steps),
            [message] * len(steps),
            [pltpu.VMEM(message[0], F32)],
            [VMEM, VMEM],
            residual,
            held,
            flops=piece_flops * len(steps) * 8,
        )

    (copies,) = call(
        first_kernel,
        [line],
        [pad],
        [SMEM, SMEM, VMEM],
        geno_live,
        image_live,
        current,
        grant=LARGE,
    )
    for sweep in range(ITERS):
        windows = exchange(copies, FAR)
        (joined,) = call(
            functools.partial(join_kernel, width), [message], [], [VMEM], windows
        )
        received = [send(joined, step) for step in STEPS]
        if sweep == 0:
            part, held = call(
                functools.partial(project_first_kernel, far),
                [total, (own_block.shape, BF16)],
                [pltpu.SemaphoreType.DMA((CHUNKS,))],
                [pl.BlockSpec(memory_space=pl.ANY), VMEM],
                own_block,
                joined,
                grant=MEDIUM,
                flops=piece_flops,
            )
        else:
            part = project(project_own_kernel, total, (HERE,), held, joined)
        part = project(project_kernel, total, STEPS[:2], held, part, *received[:2])
        copies = project(project_last_kernel, partial, STEPS[2:], held, part, *received[2:])
        partials = exchange(copies, "feat")
        own, partner, copies = call(
            gram_kernel, [rows, rows, ((doms, 8, LANES), F32)], [], [VMEM], partials
        )
        grams = exchange(copies, DOM)
        residual, made = call(
            functools.partial(residual_kernel, participants, far),
            [((K, row_count), BF16), message],
            [pltpu.VMEM(message[0], F32)],
            [VMEM] * 4,
            grams,
            own,
            partner,
            held,
        )
        first = send(made, STEPS[2])
        made = messages(residual, held, STEPS[:2])
        received = [send(item, step) for item, step in zip(made, STEPS[:2])]
        kernel = functools.partial(kept_kernel, far)
        (kept,) = call(
            kernel, [(message[0], F32)], [], [VMEM] * 3, residual, held, first, flops=piece_flops * 8
        )
        kernel = functools.partial(fold_kernel, width)
        (copies,) = call(kernel, [line], [], [VMEM] * 3, kept, *received)
        shares = exchange(copies, FAR)
        operands = (geno_live, image_live, shares, current)
        specs = [SMEM, SMEM, VMEM, VMEM]
        if sweep < ITERS - 1:
            kernel = functools.partial(update_kernel, step_size)
            current, copies = call(kernel, [(current.shape, F32), line], [pad], specs, *operands)
        else:
            kernel = functools.partial(last_kernel, step_size)
            (current,) = call(kernel, [(current.shape, F32)], [], specs, *operands)
    return current[None]


def solution(mesh):
    ys = 4
    shape = (mesh.shape["dom"] // ys // 2, 2, ys // 2, 2, mesh.shape["feat"])
    split = Mesh(mesh.devices.reshape(shape), AXES)
    placed = (P(DOM, "feat", None), P("feat", None, DOM), P(), P())
    return jax.shard_map(
        body, mesh=split, in_specs=placed, out_specs=P("feat", None, DOM), check_vma=False
    )
```

```python
import functools
import jax
import jax.numpy as jnp
from jax import lax
from jax.experimental import pallas as pl
from jax.experimental.pallas import tpu as pltpu
from jax.sharding import Mesh
from jax.sharding import PartitionSpec as P

GX = 100000
GY = 50000
K = 32
ITERS = 2
LANES = 128
STEPS = ((1, 0), (0, 1), (1, 1))
HERE = (0, 0)
FAR = ("za", "ya")
DOM = ("za", "zb", "ya", "yb")
AXES = DOM + ("feat",)
CHUNKS = 8
GROUP = 8
step_rate = 0.1
jitter = 1e-05

VMEM = pl.BlockSpec(memory_space=pltpu.VMEM)
SMEM = pl.BlockSpec(memory_space=pltpu.SMEM)
SMALL = 24 * 1024 * 1024
MEDIUM = 36 * 1024 * 1024
LARGE = 60 * 1024 * 1024
HIGH = lax.Precision.HIGHEST
F32 = jnp.float32
BF16 = jnp.bfloat16


def padded(width):
    return -(-width // LANES) * LANES


def window(width):
    return padded(width + LANES - 16)


def base_of(index, width):
    return (index * width) // LANES * LANES


def offset_of(index, width):
    return lax.rem(index * width, LANES)


def moved(values, source, target, width):
    size = values.shape[1]
    lane = lax.broadcasted_iota(jnp.int32, values.shape, 1)
    values = jnp.where((lane >= source) & (lane < source + width), values, 0.0)
    return pltpu.roll(values, lax.rem(target - source + size, size), 1)


def far_index():
    return lax.axis_index("za") * lax.axis_size("ya") + lax.axis_index("ya")


def shard_index(part, step):
    ya = lax.axis_size("ya")
    z = part // ya * 2 + lax.rem(lax.axis_index("zb") + step[0], 2)
    y = part % ya * 2 + lax.rem(lax.axis_index("yb") + step[1], 2)
    return z * (2 * ya) + y


def route(step, zs, ys, feats):
    def partner(place, size, odd, flip):
        return (place + (1 if place % 2 == odd else -1)) % size if flip else place

    pairs = []
    for z in range(zs):
        for y in range(ys):
            for feat in range(feats):
                odd = feat % 2
                to_z = partner(z, zs, odd, step[0])
                to_y = partner(y, ys, odd, step[1])
                pairs.append(((z * ys + y) * feats + feat, (to_z * ys + to_y) * feats + feat))
    return pairs


def send(message, step):
    zs, ys = 2 * lax.axis_size("za"), 2 * lax.axis_size("ya")
    return lax.ppermute(message, AXES, route(step, zs, ys, lax.axis_size("feat")))


def columns_of(part, step, width):
    begin = shard_index(part, step) * width
    base = pl.multiple_of(lax.div(begin, LANES) * LANES, LANES)
    return pl.ds(base, window(width)), lax.rem(begin, LANES)


def is_geno():
    return lax.axis_index("feat") < lax.axis_size("feat") // 2


def lane_mask(geno_live, image_live, width):
    slot = lax.rem(lax.axis_index("feat"), lax.axis_size("feat") // 2)
    live = jnp.where(is_geno(), geno_live[slot], image_live[slot])
    shard = lax.axis_index(DOM)
    column = lax.broadcasted_iota(jnp.int32, (K, width), 1) + shard * width
    return (column < live).astype(F32)


def spread(masked, width, pad, copies):
    pad[...] = jnp.zeros(pad.shape, F32)
    pad[:, :width] = masked
    shift = offset_of(far_index(), width)
    rounded = pltpu.roll(pad[...], shift, 1).astype(BF16)
    for copy in range(copies.shape[0]):
        copies[copy] = rounded


def first_kernel(geno_live, image_live, weights, copies, mask, pad):
    width = weights.shape[1]
    mask[...] = lane_mask(geno_live, image_live, width)
    spread(weights[...] * mask[...], width, pad, copies)


def join_kernel(width, windows, joined):
    size = windows.shape[2]
    joined[...] = jnp.zeros(joined.shape, BF16)
    for part in range(windows.shape[0]):
        base = base_of(part, width)
        joined[:, base : base + size] += windows[part]


def projected(far, steps, pieces, features, total):
    width = features.shape[1] // (far * 4)
    size = window(width)
    for step, piece in zip(steps, pieces):
        for part in range(far):
            columns, begin = columns_of(part, step, width)
            start = base_of(part, width)
            weights = piece[:, start : start + size].astype(F32)
            weights = moved(weights, part * width % LANES, begin, width).astype(BF16)
            product = lax.dot_general(
                features[:, columns],
                weights,
                (((1,), (1,)), ((), ())),
                preferred_element_type=F32,
            )
            total = product if total is None else total + product
    return total


def project_first_kernel(far, features, joined, total, held, arrived):
    rows = features.shape[0] // CHUNKS
    copies = []
    for chunk in range(CHUNKS):
        place = pl.ds(chunk * rows, rows)
        copies.append(
            pltpu.make_async_copy(features.at[place], held.at[place], arrived.at[chunk])
        )
        copies[-1].start()
    for copy in copies:
        copy.wait()
    total[...] = projected(far, (HERE,), (joined,), held, None)


def project_own_kernel(far, steps, features, *rest):
    *pieces, total = rest
    total[...] = projected(far, steps, pieces, features, None)


def project_kernel(far, steps, features, before, *rest):
    *pieces, total = rest
    total[...] = projected(far, steps, pieces, features, before[...])


def project_last_kernel(far, steps, features, before, *rest):
    *pieces, copies = rest
    total = projected(far, steps, pieces, features, before[...]).T
    for copy in range(copies.shape[0]):
        copies[copy] = total


def gram_kernel(partials, own, partner, copies):
    half = partials.shape[0] // 2
    geno = partials[0]
    image = partials[half]
    for block in range(1, half):
        geno += partials[block]
        image += partials[half + block]
    geno *= GX ** (-0.5)
    image *= GY ** (-0.5)
    own[...] = jnp.where(is_geno(), geno, image)
    other = jnp.where(is_geno(), image, geno)
    partner[...] = other
    tiled = jnp.concatenate([other] * (LANES // K), axis=0)
    gram = lax.dot_general(
        other, tiled, (((1,), (1,)), ((), ())), precision=HIGH, preferred_element_type=F32
    )
    lane = lax.broadcasted_iota(jnp.int32, (8, LANES), 1)
    packed = jnp.zeros((8, LANES), F32)
    for part in range(LANES // K):
        packed = jnp.where(lane // K == part, gram[8 * part : 8 * part + 8], packed)
    for copy in range(copies.shape[0]):
        copies[copy] = packed


def message_row(far, step, residual, features, row):
    width = features.shape[1] // (far * 4)
    size = window(width)
    row[...] = jnp.zeros(row.shape, F32)
    for part in range(far):
        columns, begin = columns_of(part, step, width)
        piece = lax.dot_general(
            residual[...],
            features[:, columns],
            (((1,), (0,)), ((), ())),
            preferred_element_type=F32,
        )
        start = base_of(part, width)
        row[:, start : start + size] += moved(piece, begin, part * width % LANES, width)


def residual_kernel(participants, far, grams, own, partner, features, residual, message, row_sum):
    total = grams[0]
    for part in range(1, grams.shape[0]):
        total += grams[part]
    rows = [total] + [pltpu.roll(total, LANES - K * part, 1) for part in range(1, LANES // K)]
    row = lax.broadcasted_iota(jnp.int32, (K, LANES), 0)
    lane = lax.broadcasted_iota(jnp.int32, (K, LANES), 1)
    covariance = jnp.concatenate(rows, axis=0) / participants
    covariance += jnp.where(lane == row, jitter, 0.0)
    state = jnp.where(lane < K, covariance, jnp.where(lane == row + K, 1.0, 0.0))
    for base in range(0, K, GROUP):
        columns = [
            jnp.broadcast_to(state[:, base + i : base + i + 1], state.shape) for i in range(GROUP)
        ]
        rows = [state[base + i : base + i + 1, :] for i in range(GROUP)]
        for i in range(GROUP):
            step = base + i
            inverse = 1.0 / columns[i][step : step + 1, :]
            below = jnp.where(row > step, columns[i], 0.0)
            for later in range(i + 1, GROUP):
                ratio = columns[i][base + later : base + later + 1, :] * inverse
                columns[later] = columns[later] - below * ratio
                rows[later] = rows[later] - rows[i] * ratio
            state = state - below * (rows[i] * inverse)
    pivots = jnp.sum(jnp.where(lane == row, state, 0.0), axis=1, keepdims=True)
    scaled = state * lax.rsqrt(pivots)
    inverse = pltpu.roll(scaled, LANES - K, 1)[:, :K]
    target = lax.dot_general(
        inverse, partner[...], (((1,), (0,)), ((), ())), precision=HIGH, preferred_element_type=F32
    )
    residual[...] = (own[...] - target).astype(BF16)
    message_row(far, STEPS[2], residual, features, row_sum)
    message[...] = row_sum[...].astype(BF16)


def message_kernel(far, steps, residual, features, *rest):
    *messages, row = rest
    for step, message in zip(steps, messages):
        message_row(far, step, residual, features, row)
        message[...] = row[...].astype(BF16)


def kept_kernel(far, residual, features, received, kept):
    message_row(far, HERE, residual, features, kept)
    kept[...] += received[...].astype(F32)


def fold_kernel(width, own, *rest):
    *received, windows = rest
    total = own[...]
    for message in received:
        total += message[...].astype(F32)
    total = total.astype(BF16)
    size = windows.shape[2]
    for part in range(windows.shape[0]):
        start = base_of(part, width)
        windows[part] = total[:, start : start + size]


def updated_weights(step_size, mask, windows, weights):
    width = weights.shape[1]
    total = windows[0].astype(F32)
    for part in range(1, windows.shape[0]):
        total += windows[part].astype(F32)
    size = windows.shape[2]
    shift = lax.rem(size - offset_of(far_index(), width), size)
    gradient = pltpu.roll(total, shift, 1)[:, :width]
    return mask[...] * (weights[...] - step_size * gradient)


def update_kernel(step_size, mask, windows, weights, updated, copies, pad):
    fresh = updated_weights(step_size, mask, windows, weights)
    updated[...] = fresh
    spread(fresh, weights.shape[1], pad, copies)


def last_kernel(step_size, mask, windows, weights, updated):
    updated[...] = updated_weights(step_size, mask, windows, weights)


def call(kernel, outs, scratch, specs, *operands, grant=SMALL, flops=0):
    shapes = tuple(jax.ShapeDtypeStruct(*out) for out in outs)
    return pl.pallas_call(
        kernel,
        out_shape=shapes,
        in_specs=specs,
        out_specs=tuple(VMEM for _ in shapes),
        scratch_shapes=list(scratch),
        compiler_params=pltpu.CompilerParams(vmem_limit_bytes=grant),
        cost_estimate=pl.CostEstimate(flops=flops, bytes_accessed=1 << 10, transcendentals=0),
    )(*operands)


def exchange(copies, axis):
    return lax.all_to_all(copies, axis, 0, 0, tiled=True)


def body(features, weights, geno_live, image_live):
    row_count = features.shape[0]
    own_block = features[:, 0, :]
    current = weights[0]
    width = current.shape[1]
    size = window(width)
    doms = lax.axis_size(DOM)
    far = lax.axis_size(FAR)
    feats = lax.axis_size("feat")
    participants = row_count * doms
    step_size = step_rate * participants ** (-0.5)

    joined_size = base_of(far - 1, width) + size
    pad = pltpu.VMEM((K, size), F32)
    line = ((far, K, size), BF16)
    message = ((K, joined_size), BF16)
    rows = ((K, row_count), F32)
    total = ((row_count, K), F32)
    partial = ((feats, K, row_count), F32)
    piece_flops = 2 * row_count * K * joined_size

    def project(kernel, out, steps, *operands):
        kernel = functools.partial(kernel, far, steps)
        flops = piece_flops * len(steps)
        return call(kernel, [out], [], [VMEM] * len(operands), *operands, flops=flops)[0]

    def messages(residual, held, steps):
        return call(
            functools.partial(message_kernel, far, steps),
            [message] * len(steps),
            [pltpu.VMEM(message[0], F32)],
            [VMEM, VMEM],
            residual,
            held,
            flops=piece_flops * len(steps) * 8,
        )

    copies, mask = call(
        first_kernel,
        [line, (current.shape, F32)],
        [pad],
        [SMEM, SMEM, VMEM],
        geno_live,
        image_live,
        current,
        grant=LARGE,
    )
    for sweep in range(ITERS):
        windows = exchange(copies, FAR)
        (joined,) = call(
            functools.partial(join_kernel, width), [message], [], [VMEM], windows
        )
        received = [send(joined, step) for step in STEPS]
        if sweep == 0:
            part, held = call(
                functools.partial(project_first_kernel, far),
                [total, (own_block.shape, BF16)],
                [pltpu.SemaphoreType.DMA((CHUNKS,))],
                [pl.BlockSpec(memory_space=pl.ANY), VMEM],
                own_block,
                joined,
                grant=MEDIUM,
                flops=piece_flops,
            )
        else:
            part = project(project_own_kernel, total, (HERE,), held, joined)
        part = project(project_kernel, total, STEPS[:2], held, part, *received[:2])
        copies = project(project_last_kernel, partial, STEPS[2:], held, part, *received[2:])
        partials = exchange(copies, "feat")
        own, partner, copies = call(
            gram_kernel, [rows, rows, ((doms, 8, LANES), F32)], [], [VMEM], partials
        )
        grams = exchange(copies, DOM)
        residual, made = call(
            functools.partial(residual_kernel, participants, far),
            [((K, row_count), BF16), message],
            [pltpu.VMEM(message[0], F32)],
            [VMEM] * 4,
            grams,
            own,
            partner,
            held,
        )
        first = send(made, STEPS[2])
        made = messages(residual, held, STEPS[:2])
        received = [send(item, step) for item, step in zip(made, STEPS[:2])]
        kernel = functools.partial(kept_kernel, far)
        (kept,) = call(
            kernel, [(message[0], F32)], [], [VMEM] * 3, residual, held, first, flops=piece_flops * 8
        )
        kernel = functools.partial(fold_kernel, width)
        (copies,) = call(kernel, [line], [], [VMEM] * 3, kept, *received)
        shares = exchange(copies, FAR)
        operands = (mask, shares, current)
        specs = [VMEM] * 3
        if sweep < ITERS - 1:
            kernel = functools.partial(update_kernel, step_size)
            current, copies = call(kernel, [(current.shape, F32), line], [pad], specs, *operands)
        else:
            kernel = functools.partial(last_kernel, step_size)
            (current,) = call(kernel, [(current.shape, F32)], [], specs, *operands)
    return current[None]


def solution(mesh):
    ys = 4
    shape = (mesh.shape["dom"] // ys // 2, 2, ys // 2, 2, mesh.shape["feat"])
    split = Mesh(mesh.devices.reshape(shape), AXES)
    placed = (P(DOM, "feat", None), P("feat", None, DOM), P(), P())
    return jax.shard_map(
        body, mesh=split, in_specs=placed, out_specs=P("feat", None, DOM), check_vma=False
    )
```

```python
import functools
import jax
import jax.numpy as jnp
from jax import lax
from jax.experimental import pallas as pl
from jax.experimental.pallas import tpu as pltpu
from jax.sharding import Mesh
from jax.sharding import PartitionSpec as P

GX = 100000
GY = 50000
K = 32
ITERS = 2
LANES = 128
STEPS = ((0, 1), (1, 0), (1, 1))
HERE = (0, 0)
FAR = ("za", "ya")
DOM = ("za", "zb", "ya", "yb")
AXES = DOM + ("feat",)
CHUNKS = 8
GROUP = 8
step_rate = 0.1
jitter = 1e-05

VMEM = pl.BlockSpec(memory_space=pltpu.VMEM)
SMEM = pl.BlockSpec(memory_space=pltpu.SMEM)
SMALL = 24 * 1024 * 1024
MEDIUM = 36 * 1024 * 1024
LARGE = 60 * 1024 * 1024
HIGH = lax.Precision.HIGHEST
F32 = jnp.float32
BF16 = jnp.bfloat16


def padded(width):
    return -(-width // LANES) * LANES


def window(width):
    return padded(width + LANES - 16)


def base_of(index, width):
    return (index * width) // LANES * LANES


def offset_of(index, width):
    return lax.rem(index * width, LANES)


def moved(values, source, target, width):
    size = values.shape[1]
    lane = lax.broadcasted_iota(jnp.int32, values.shape, 1)
    values = jnp.where((lane >= source) & (lane < source + width), values, 0.0)
    return pltpu.roll(values, lax.rem(target - source + size, size), 1)


def far_index():
    return lax.axis_index("za") * lax.axis_size("ya") + lax.axis_index("ya")


def shard_index(part, step):
    ya = lax.axis_size("ya")
    z = part // ya * 2 + lax.rem(lax.axis_index("zb") + step[0], 2)
    y = part % ya * 2 + lax.rem(lax.axis_index("yb") + step[1], 2)
    return z * (2 * ya) + y


def route(step, zs, ys, feats):
    def partner(place, size, odd, flip):
        return (place + (1 if place % 2 == odd else -1)) % size if flip else place

    pairs = []
    for z in range(zs):
        for y in range(ys):
            for feat in range(feats):
                odd = feat % 2
                to_z = partner(z, zs, odd, step[0])
                to_y = partner(y, ys, odd, step[1])
                pairs.append(((z * ys + y) * feats + feat, (to_z * ys + to_y) * feats + feat))
    return pairs


def send(message, step):
    zs, ys = 2 * lax.axis_size("za"), 2 * lax.axis_size("ya")
    return lax.ppermute(message, AXES, route(step, zs, ys, lax.axis_size("feat")))


def columns_of(part, step, width):
    begin = shard_index(part, step) * width
    base = pl.multiple_of(lax.div(begin, LANES) * LANES, LANES)
    return pl.ds(base, window(width)), lax.rem(begin, LANES)


def is_geno():
    return lax.axis_index("feat") < lax.axis_size("feat") // 2


def lane_mask(geno_live, image_live, width):
    slot = lax.rem(lax.axis_index("feat"), lax.axis_size("feat") // 2)
    live = jnp.where(is_geno(), geno_live[slot], image_live[slot])
    shard = lax.axis_index(DOM)
    column = lax.broadcasted_iota(jnp.int32, (K, width), 1) + shard * width
    return (column < live).astype(F32)


def spread(masked, width, pad, copies):
    pad[...] = jnp.zeros(pad.shape, F32)
    pad[:, :width] = masked
    shift = offset_of(far_index(), width)
    rounded = pltpu.roll(pad[...], shift, 1).astype(BF16)
    for copy in range(copies.shape[0]):
        copies[copy] = rounded


def first_kernel(geno_live, image_live, weights, copies, mask, pad):
    width = weights.shape[1]
    mask[...] = lane_mask(geno_live, image_live, width)
    spread(weights[...] * mask[...], width, pad, copies)


def join_kernel(width, windows, joined):
    size = windows.shape[2]
    joined[...] = jnp.zeros(joined.shape, BF16)
    for part in range(windows.shape[0]):
        base = base_of(part, width)
        joined[:, base : base + size] += windows[part]


def projected(far, steps, pieces, features, total):
    width = features.shape[1] // (far * 4)
    size = window(width)
    for step, piece in zip(steps, pieces):
        for part in range(far):
            columns, begin = columns_of(part, step, width)
            start = base_of(part, width)
            weights = piece[:, start : start + size].astype(F32)
            weights = moved(weights, part * width % LANES, begin, width).astype(BF16)
            product = lax.dot_general(
                weights,
                features[:, columns],
                (((1,), (1,)), ((), ())),
                preferred_element_type=F32,
            )
            total = product if total is None else total + product
    return total


def project_first_kernel(far, features, joined, total, held, arrived):
    rows = features.shape[0] // CHUNKS
    copies = []
    for chunk in range(CHUNKS):
        place = pl.ds(chunk * rows, rows)
        copies.append(
            pltpu.make_async_copy(features.at[place], held.at[place], arrived.at[chunk])
        )
        copies[-1].start()
    for copy in copies:
        copy.wait()
    total[...] = projected(far, (HERE,), (joined,), held, None)


def project_own_kernel(far, steps, features, *rest):
    *pieces, total = rest
    total[...] = projected(far, steps, pieces, features, None)


def project_kernel(far, steps, features, before, *rest):
    *pieces, total = rest
    total[...] = projected(far, steps, pieces, features, before[...])


def project_last_kernel(far, steps, features, before, *rest):
    *pieces, copies = rest
    total = projected(far, steps, pieces, features, before[...])
    for copy in range(copies.shape[0]):
        copies[copy] = total


def gram_kernel(partials, own, partner, copies):
    half = partials.shape[0] // 2
    geno = partials[0]
    image = partials[half]
    for block in range(1, half):
        geno += partials[block]
        image += partials[half + block]
    geno *= GX ** (-0.5)
    image *= GY ** (-0.5)
    own[...] = jnp.where(is_geno(), geno, image)
    other = jnp.where(is_geno(), image, geno)
    partner[...] = other
    tiled = jnp.concatenate([other] * (LANES // K), axis=0)
    gram = lax.dot_general(
        other, tiled, (((1,), (1,)), ((), ())), precision=HIGH, preferred_element_type=F32
    )
    lane = lax.broadcasted_iota(jnp.int32, (8, LANES), 1)
    packed = jnp.zeros((8, LANES), F32)
    for part in range(LANES // K):
        packed = jnp.where(lane // K == part, gram[8 * part : 8 * part + 8], packed)
    for copy in range(copies.shape[0]):
        copies[copy] = packed


def message_row(far, step, residual, features, row):
    width = features.shape[1] // (far * 4)
    size = window(width)
    row[...] = jnp.zeros(row.shape, F32)
    for part in range(far):
        columns, begin = columns_of(part, step, width)
        piece = lax.dot_general(
            residual[...],
            features[:, columns],
            (((1,), (0,)), ((), ())),
            preferred_element_type=F32,
        )
        start = base_of(part, width)
        row[:, start : start + size] += moved(piece, begin, part * width % LANES, width)


def residual_kernel(participants, far, grams, own, partner, features, residual, message, row_sum):
    total = grams[0]
    for part in range(1, grams.shape[0]):
        total += grams[part]
    rows = [total] + [pltpu.roll(total, LANES - K * part, 1) for part in range(1, LANES // K)]
    row = lax.broadcasted_iota(jnp.int32, (K, LANES), 0)
    lane = lax.broadcasted_iota(jnp.int32, (K, LANES), 1)
    covariance = jnp.concatenate(rows, axis=0) / participants
    covariance += jnp.where(lane == row, jitter, 0.0)
    state = jnp.where(lane < K, covariance, jnp.where(lane == row + K, 1.0, 0.0))
    for base in range(0, K, GROUP):
        columns = [
            jnp.broadcast_to(state[:, base + i : base + i + 1], state.shape) for i in range(GROUP)
        ]
        rows = [state[base + i : base + i + 1, :] for i in range(GROUP)]
        for i in range(GROUP):
            step = base + i
            inverse = 1.0 / columns[i][step : step + 1, :]
            below = jnp.where(row > step, columns[i], 0.0)
            for later in range(i + 1, GROUP):
                ratio = columns[i][base + later : base + later + 1, :] * inverse
                columns[later] = columns[later] - below * ratio
                rows[later] = rows[later] - rows[i] * ratio
            state = state - below * (rows[i] * inverse)
    pivots = jnp.sum(jnp.where(lane == row, state, 0.0), axis=1, keepdims=True)
    scaled = state * lax.rsqrt(pivots)
    inverse = pltpu.roll(scaled, LANES - K, 1)[:, :K]
    target = lax.dot_general(
        inverse, partner[...], (((1,), (0,)), ((), ())), precision=HIGH, preferred_element_type=F32
    )
    residual[...] = (own[...] - target).astype(BF16)
    message_row(far, STEPS[2], residual, features, row_sum)
    message[...] = row_sum[...].astype(BF16)


def message_kernel(far, steps, residual, features, *rest):
    *messages, row = rest
    for step, message in zip(steps, messages):
        message_row(far, step, residual, features, row)
        message[...] = row[...].astype(BF16)


def kept_kernel(far, residual, features, received, kept):
    message_row(far, HERE, residual, features, kept)
    kept[...] += received[...].astype(F32)


def fold_kernel(width, own, *rest):
    *received, windows = rest
    total = own[...]
    for message in received:
        total += message[...].astype(F32)
    total = total.astype(BF16)
    size = windows.shape[2]
    for part in range(windows.shape[0]):
        start = base_of(part, width)
        windows[part] = total[:, start : start + size]


def updated_weights(step_size, mask, windows, weights):
    width = weights.shape[1]
    total = windows[0].astype(F32)
    for part in range(1, windows.shape[0]):
        total += windows[part].astype(F32)
    size = windows.shape[2]
    shift = lax.rem(size - offset_of(far_index(), width), size)
    gradient = pltpu.roll(total, shift, 1)[:, :width]
    return mask[...] * (weights[...] - step_size * gradient)


def update_kernel(step_size, mask, windows, weights, updated, copies, pad):
    fresh = updated_weights(step_size, mask, windows, weights)
    updated[...] = fresh
    spread(fresh, weights.shape[1], pad, copies)


def last_kernel(step_size, mask, windows, weights, updated):
    updated[...] = updated_weights(step_size, mask, windows, weights)


def call(kernel, outs, scratch, specs, *operands, grant=SMALL, flops=0):
    shapes = tuple(jax.ShapeDtypeStruct(*out) for out in outs)
    return pl.pallas_call(
        kernel,
        out_shape=shapes,
        in_specs=specs,
        out_specs=tuple(VMEM for _ in shapes),
        scratch_shapes=list(scratch),
        compiler_params=pltpu.CompilerParams(vmem_limit_bytes=grant),
        cost_estimate=pl.CostEstimate(flops=flops, bytes_accessed=1 << 10, transcendentals=0),
    )(*operands)


def exchange(copies, axis):
    return lax.all_to_all(copies, axis, 0, 0, tiled=True)


def body(features, weights, geno_live, image_live):
    row_count = features.shape[0]
    own_block = features[:, 0, :]
    current = weights[0]
    width = current.shape[1]
    size = window(width)
    doms = lax.axis_size(DOM)
    far = lax.axis_size(FAR)
    feats = lax.axis_size("feat")
    participants = row_count * doms
    step_size = step_rate * participants ** (-0.5)

    joined_size = base_of(far - 1, width) + size
    pad = pltpu.VMEM((K, size), F32)
    line = ((far, K, size), BF16)
    message = ((K, joined_size), BF16)
    rows = ((K, row_count), F32)
    total = ((K, row_count), F32)
    partial = ((feats, K, row_count), F32)
    piece_flops = 2 * row_count * K * joined_size

    def project(kernel, out, steps, *operands):
        kernel = functools.partial(kernel, far, steps)
        flops = piece_flops * len(steps)
        return call(kernel, [out], [], [VMEM] * len(operands), *operands, flops=flops)[0]

    def messages(residual, held, steps):
        return call(
            functools.partial(message_kernel, far, steps),
            [message] * len(steps),
            [pltpu.VMEM(message[0], F32)],
            [VMEM, VMEM],
            residual,
            held,
            flops=piece_flops * len(steps) * 8,
        )

    copies, mask = call(
        first_kernel,
        [line, (current.shape, F32)],
        [pad],
        [SMEM, SMEM, VMEM],
        geno_live,
        image_live,
        current,
        grant=LARGE,
    )
    for sweep in range(ITERS):
        windows = exchange(copies, FAR)
        (joined,) = call(
            functools.partial(join_kernel, width), [message], [], [VMEM], windows
        )
        received = [send(joined, step) for step in STEPS]
        if sweep == 0:
            part, held = call(
                functools.partial(project_first_kernel, far),
                [total, (own_block.shape, BF16)],
                [pltpu.SemaphoreType.DMA((CHUNKS,))],
                [pl.BlockSpec(memory_space=pl.ANY), VMEM],
                own_block,
                joined,
                grant=MEDIUM,
                flops=piece_flops,
            )
        else:
            part = project(project_own_kernel, total, (HERE,), held, joined)
        part = project(project_kernel, total, STEPS[:2], held, part, *received[:2])
        copies = project(project_last_kernel, partial, STEPS[2:], held, part, *received[2:])
        partials = exchange(copies, "feat")
        own, partner, copies = call(
            gram_kernel, [rows, rows, ((doms, 8, LANES), F32)], [], [VMEM], partials
        )
        grams = exchange(copies, DOM)
        residual, made = call(
            functools.partial(residual_kernel, participants, far),
            [((K, row_count), BF16), message],
            [pltpu.VMEM(message[0], F32)],
            [VMEM] * 4,
            grams,
            own,
            partner,
            held,
        )
        first = send(made, STEPS[2])
        received = []
        for step in STEPS[1::-1]:
            (made,) = messages(residual, held, (step,))
            received.append(send(made, step))
        kernel = functools.partial(kept_kernel, far)
        (kept,) = call(
            kernel, [(message[0], F32)], [], [VMEM] * 3, residual, held, first, flops=piece_flops * 8
        )
        kernel = functools.partial(fold_kernel, width)
        (copies,) = call(kernel, [line], [], [VMEM] * 3, kept, *received)
        shares = exchange(copies, FAR)
        operands = (mask, shares, current)
        specs = [VMEM] * 3
        if sweep < ITERS - 1:
            kernel = functools.partial(update_kernel, step_size)
            current, copies = call(kernel, [(current.shape, F32), line], [pad], specs, *operands)
        else:
            kernel = functools.partial(last_kernel, step_size)
            (current,) = call(kernel, [(current.shape, F32)], [], specs, *operands)
    return current[None]


def solution(mesh):
    ys = 4
    shape = (mesh.shape["dom"] // ys // 2, 2, ys // 2, 2, mesh.shape["feat"])
    split = Mesh(mesh.devices.reshape(shape), AXES)
    placed = (P(DOM, "feat", None), P("feat", None, DOM), P(), P())
    return jax.shard_map(
        body, mesh=split, in_specs=placed, out_specs=P("feat", None, DOM), check_vma=False
    )
```
